512 devices in a mesh: blk: 32 (over y_lo, z), dp: 16 (over y_hi, x, core).
Axes of the slice: x: 4, y: 8 (y_hi: 2, y_lo: 4; y = y_hi * 4 + y_lo), z: 8, core: 2. Of those that a mesh axis runs over, the one named last changes fastest.
Arguments:
- image_embed: bfloat16 [131072, 1152], P(('blk', 'dp')), may hold values from -0.29882812 to 0.29882812
- text_embed: bfloat16 [131072, 1152], P(('blk', 'dp')), may hold values from -0.29882812 to 0.29882812
- log_temp: float32 [1], replicated, may hold values from 1.1 to 2.3
- bias: float32 [1], replicated, may hold values from -4 to -1
Outputs:
- loss: float32 [1], replicated
- grad_logt: float32 [1], replicated
- grad_bias: float32 [1], replicated
- grad_image: float32 [131072, 1152], P(('blk', 'dp'))
- grad_text: float32 [131072, 1152], P(('blk', 'dp'))
The draws below stay inside these ranges and needn't reach their ends.
All inputs are finite; a program needn't handle non-finite values.
Results may differ from the reference program's by a relative error of at most 0.0033.
The reference program's roundings to bfloat16 on the way count: a program that leaves them out, or rounds other values in their place, can miss the bound.
Values may be sent and summed in bfloat16 or wider, within the bound.
No kernel may reach another device: no remote copies, remote signals or barrier semaphores. Data moves between devices by JAX's collectives and lax.ppermute only.
A program may use at most 64 MiB of HBM per device.

```python
import jax
import jax.numpy as jnp
from jax import lax

D = 1152
ROWS = 256
ROT = 8
HALF = 4
PAIRS = 131072
N_BLK = 32
N_DP = 16


def level_of(key, dims, split, smallest, high):
    loudness, own = 1.0, jax.random.fold_in(key, 6)
    for position, shards_of in split:
        steps = jnp.exp(jax.random.uniform(jax.random.fold_in(own, position), (shards_of,), jnp.float32, smallest / len(split), high / len(split)))
        loudness = loudness * jnp.repeat(steps, dims[position] // shards_of).reshape([-1 if axis == position else 1 for axis in range(len(dims))])
    return loudness


def noise(own_key, extent, spread, reach, shards=(), kind=jnp.bfloat16):
    factor_of = level_of(own_key, extent, shards, -0.22, 0.18) if shards else 1.0
    array = jax.random.normal(own_key, extent, jnp.float32) * spread * factor_of
    return jnp.minimum(jnp.maximum(array, -reach), reach).astype(kind)


def setup_inputs(seed: int = 0) -> dict:
    splits = jax.random.split(jax.random.key(seed), 5)
    image_embed = noise(splits[0], (PAIRS, D), 0.05, 0.29882812, ((0, 512),))
    text_embed = noise(splits[1], (PAIRS, D), 0.05, 0.29882812, ((0, 512),))
    log_temp = jnp.clip(jax.random.uniform(splits[2], (1,), jnp.float32, 1.1, 2.3), 1.1, 2.3)
    bias = jnp.clip(jax.random.uniform(splits[3], (1,), jnp.float32, -4.0, -1.0), -4.0, -1.0)
    return dict(image_embed=image_embed, text_embed=text_embed, log_temp=log_temp, bias=bias)


def normalize(x):
    xf = x.astype(jnp.float32)
    inv = lax.rsqrt(lax.optimization_barrier(jnp.sum(xf * xf, axis=-1, keepdims=True)) + 1e-06)
    return (xf * inv, inv)

def denormalize(grad, unit, inv):
    return inv * (grad - unit * lax.optimization_barrier(jnp.sum(unit * grad, axis=-1, keepdims=True)))

def reference(image_embed, text_embed, log_temp, bias):
    unit_i, inv_i = normalize(image_embed)
    unit_t, inv_t = normalize(text_embed)
    img4 = unit_i.astype(jnp.bfloat16).astype(jnp.float32).reshape(N_BLK, N_DP, ROWS, D)
    txt4 = unit_t.astype(jnp.bfloat16).astype(jnp.float32).reshape(N_BLK, N_DP, ROWS, D)
    temp = jnp.exp(log_temp[0])
    shift_b = bias[0]
    eye = jnp.eye(ROWS, dtype=jnp.float32)
    total = jnp.float32(0.0)
    dtemp = jnp.float32(0.0)
    dbias = jnp.float32(0.0)
    gimg = jnp.zeros((N_BLK, N_DP, ROWS, D), jnp.float32)
    gtxt = jnp.zeros((N_BLK, N_DP, ROWS, D), jnp.float32)
    for step in range(ROT):
        offset = step - HALF
        other = jnp.roll(txt4, -offset, axis=0)
        dots = jnp.einsum('bdrc,bdsc->bdrs', img4, other)
        logit = temp * dots + shift_b
        if offset == 0:
            sign = 2.0 * eye - 1.0
        else:
            sign = -jnp.ones_like(eye)
        total = total - jnp.sum(jax.nn.log_sigmoid(sign * logit))
        dl = -sign * jax.nn.sigmoid(-sign * logit)
        dtemp = dtemp + jnp.sum(dl * temp * dots)
        dbias = dbias + jnp.sum(dl)
        g = (temp * dl).astype(jnp.bfloat16).astype(jnp.float32)
        gimg = gimg + jnp.einsum('bdrs,bdsc->bdrc', g, other)
        part = jnp.einsum('bdrs,bdrc->bdsc', g, img4)
        gtxt = gtxt + jnp.roll(part, offset, axis=0)
    grad_image = denormalize(gimg.reshape(PAIRS, D), unit_i, inv_i)
    grad_text = denormalize(gtxt.reshape(PAIRS, D), unit_t, inv_t)
    return ((total / PAIRS).reshape(1), (dtemp / PAIRS).reshape(1), (dbias / PAIRS).reshape(1), grad_image, grad_text)
```

```python
import functools

import jax
import jax.numpy as jnp
from jax import lax
from jax.experimental import pallas as pl
from jax.experimental.pallas import tpu as pltpu
from jax.sharding import PartitionSpec as P

F32, BF16 = jnp.float32, jnp.bfloat16


def shifted(array, by):
    length = lax.axis_size("blk")
    return lax.ppermute(array, "blk", [(i, (i + by) % length) for i in range(length)])


def normal(raw):
    xf = raw.astype(F32)
    inv = lax.rsqrt(jnp.sum(xf * xf, axis=-1, keepdims=True) + 1e-06)
    return xf * inv, inv


def products(a, b):
    return lax.dot_general(a, b, (((1,), (1,)), ((), ())), preferred_element_type=F32)


def sigmoid(x):
    return 1.0 / (1.0 + jnp.exp(-x))


def fold(v):
    r = jnp.sum(v.reshape(v.shape[0] // 8, 8, v.shape[1]), axis=0)
    return sum(r[:, i : i + 128] for i in range(0, v.shape[1], 128))


def add_terms(sums_ref, u, dl, scaled):
    sums_ref[0:8, :] += fold(jnp.maximum(u, 0.0) + jnp.log1p(jnp.exp(-jnp.abs(u))))
    sums_ref[8:16, :] += fold(dl * scaled)
    sums_ref[16:24, :] += fold(dl)


def off_diagonal(own, other, temp, bias, sums_ref=None):
    scaled = temp * products(own, other)
    logit = scaled + bias
    dl = sigmoid(logit)
    if sums_ref is not None:
        add_terms(sums_ref, logit, dl, scaled)
    return (temp * dl).astype(BF16)


def own_kernel(temp_ref, bias_ref, img_ref, txt_ref, img_n_ref, txt_n_ref, gimg_ref, gtxt_ref, sums_ref):
    temp, bias = jnp.exp(temp_ref[...]), bias_ref[...]
    img_n_ref[...] = normal(img_ref[...])[0].astype(BF16)
    txt_n_ref[...] = normal(txt_ref[...])[0].astype(BF16)
    scaled = temp * products(img_n_ref[...], txt_n_ref[...])
    logit = scaled + bias
    rows = lax.broadcasted_iota(jnp.int32, logit.shape, 0)
    cols = lax.broadcasted_iota(jnp.int32, logit.shape, 1)
    diagonal = rows == cols
    u = jnp.where(diagonal, -logit, logit)
    s = sigmoid(u)
    dl = jnp.where(diagonal, -s, s)
    sums_ref[...] = jnp.zeros_like(sums_ref)
    add_terms(sums_ref, u, dl, scaled)
    g = (temp * dl).astype(BF16)
    gimg_ref[...] = jnp.dot(g, txt_n_ref[...], preferred_element_type=F32)
    gtxt_ref[...] = lax.dot_general(
        g, img_n_ref[...], (((0,), (0,)), ((), ())), preferred_element_type=F32
    )


def own_tile(temp, bias, image, text):
    block = image.shape
    return pl.pallas_call(
        own_kernel,
        out_shape=(
            jax.ShapeDtypeStruct(block, BF16),
            jax.ShapeDtypeStruct(block, BF16),
            jax.ShapeDtypeStruct(block, F32),
            jax.ShapeDtypeStruct(block, F32),
            jax.ShapeDtypeStruct((24, 128), F32),
        ),
        compiler_params=pltpu.CompilerParams(vmem_limit_bytes=24 << 20),
        name="own_tile",
    )(temp, bias, image, text)


def pair_kernel(with_older, counted, keep, *refs):
    refs = list(refs)
    temp_ref, bias_ref, img_n_ref, txt_n_ref, t_ref, i_ref, gimg_in, gtxt_in = refs[:8]
    del refs[:8]
    temp, bias = jnp.exp(temp_ref[...]), bias_ref[...]
    older = None
    sums_in = None
    if with_older:
        older = refs.pop(0)
    if counted:
        sums_in = refs.pop(0)
    gimg_ref, gtxt_ref = refs[:2]
    del refs[:2]
    sums_ref = None
    if counted:
        sums_ref = refs.pop(0)
        sums_ref[...] = sums_in[...]
    t_n = normal(t_ref[...])[0].astype(BF16)
    i_n = normal(i_ref[...])[0].astype(BF16)
    if keep:
        refs.pop(0)[...] = i_n
    g = off_diagonal(img_n_ref[...], t_n, temp, bias, sums_ref)
    gimg_ref[...] = gimg_in[...] + jnp.dot(g, t_n, preferred_element_type=F32)
    g = off_diagonal(txt_n_ref[...], i_n, temp, bias)
    gtxt_ref[...] = gtxt_in[...] + jnp.dot(g, i_n, preferred_element_type=F32)
    if older is not None:
        off_diagonal(older[...], t_n, temp, bias, sums_ref)


def pair(temp, bias, own, t, i, acc, sums=None, older=None, keep=False):
    block = t.shape
    args = [temp, bias, *own, t, i, *acc]
    outs = [jax.ShapeDtypeStruct(block, F32)] * 2
    aliases = {6: 0, 7: 1}
    if older is not None:
        args.append(older)
    if sums is not None:
        aliases[len(args)] = len(outs)
        args.append(sums)
        outs.append(jax.ShapeDtypeStruct((24, 128), F32))
    if keep:
        outs.append(jax.ShapeDtypeStruct(block, BF16))
    return pl.pallas_call(
        functools.partial(pair_kernel, older is not None, sums is not None, keep),
        out_shape=tuple(outs),
        input_output_aliases=aliases,
        compiler_params=pltpu.CompilerParams(vmem_limit_bytes=24 << 20),
        name="pair",
    )(*args)


def count_kernel(temp_ref, bias_ref, i_ref, t_ref, sums_in, sums_ref):
    temp, bias = jnp.exp(temp_ref[...]), bias_ref[...]
    sums_ref[...] = sums_in[...]
    i_n = normal(i_ref[...])[0].astype(BF16)
    t_n = normal(t_ref[...])[0].astype(BF16)
    off_diagonal(i_n, t_n, temp, bias, sums_ref)


def count(temp, bias, i, t, sums):
    return pl.pallas_call(
        count_kernel,
        out_shape=jax.ShapeDtypeStruct((24, 128), F32),
        input_output_aliases={4: 0},
        compiler_params=pltpu.CompilerParams(vmem_limit_bytes=24 << 20),
        name="count",
    )(temp, bias, i, t, sums)


def last_kernel(temp_ref, bias_ref, img_n_ref, txt_n_ref, t_ref, i_ref, gimg_in, gtxt_in, img_ref, txt_ref, gimg_ref, gtxt_ref):
    temp, bias = jnp.exp(temp_ref[...]), bias_ref[...]
    for own_n, arrived, acc, own, out in (
        (img_n_ref, t_ref, gimg_in, img_ref, gimg_ref),
        (txt_n_ref, i_ref, gtxt_in, txt_ref, gtxt_ref),
    ):
        o_n = normal(arrived[...])[0].astype(BF16)
        g = off_diagonal(own_n[...], o_n, temp, bias)
        grad = acc[...] + jnp.dot(g, o_n, preferred_element_type=F32)
        unit, inv = normal(own[...])
        out[...] = inv * (grad - unit * jnp.sum(unit * grad, axis=-1, keepdims=True))


def last(temp, bias, own, t, i, acc, image, text):
    block = t.shape
    return pl.pallas_call(
        last_kernel,
        out_shape=(jax.ShapeDtypeStruct(block, F32),) * 2,
        compiler_params=pltpu.CompilerParams(vmem_limit_bytes=24 << 20),
        name="last",
    )(temp, bias, *own, t, i, *acc, image, text)


def exchange(values, axis, masks):
    length = lax.axis_size(axis)
    got = [lax.ppermute(values, axis, [(i, i ^ m) for i in range(length)]) for m in masks]
    return functools.reduce(jnp.add, got, values)


def body(image, text, log_temp, bias):
    temp, shift = log_temp.reshape(1, 1), bias.reshape(1, 1)
    pair_count = image.shape[0] * lax.axis_size("blk") * lax.axis_size("dp")
    t, i = {}, {}
    t[0], i[0] = text, image
    for s in (1, 2, 3, 4):
        t[s] = shifted(t[s - 1], 1)
        i[-s] = shifted(i[1 - s], -1)
        if s < 4:
            i[s] = shifted(i[s - 1], 1)
            t[-s] = shifted(t[1 - s], -1)

    img_n, txt_n, *acc, sums = own_tile(temp, shift, image, text)
    own = (img_n, txt_n)
    *acc, sums, i_m1 = pair(temp, shift, own, t[1], i[-1], acc, sums, keep=True)
    *acc, sums, i_1 = pair(temp, shift, own, t[-1], i[1], acc, sums, keep=True)
    *acc, sums = pair(temp, shift, own, t[2], i[-2], acc, sums, older=i_m1)
    sums = count(temp, shift, i[-2], t[2], sums)
    *acc, sums = pair(temp, shift, own, t[-2], i[2], acc, sums, older=i_1)
    for masks, axis in (((1, 8, 9), "dp"), ((2, 4, 6), "dp"), ((8, 16, 24), "blk"), ((1, 2, 3), "blk"), ((4,), "blk")):
        sums = exchange(sums, axis, masks)
    acc = pair(temp, shift, own, t[3], i[-3], acc)
    acc = pair(temp, shift, own, t[-3], i[3], acc)
    grad_image, grad_text = last(temp, shift, own, t[4], i[-4], acc, image, text)
    totals = jnp.sum(sums.reshape(3, -1), axis=1) / pair_count
    return (totals[0:1], totals[1:2], totals[2:3], grad_image, grad_text)


def solution(mesh):
    placed = (P(("blk", "dp"), None), P(("blk", "dp"), None), P(), P())
    return jax.shard_map(
        body,
        mesh=mesh,
        in_specs=placed,
        out_specs=(P(), P(), P(), P(("blk", "dp"), None), P(("blk", "dp"), None)),
        check_vma=False,
    )
```

```python
import functools

import jax
import jax.numpy as jnp
from jax import lax
from jax.experimental import pallas as pl
from jax.experimental.pallas import tpu as pltpu
from jax.sharding import PartitionSpec as P

F32, BF16 = jnp.float32, jnp.bfloat16
COST_LAST, COST_PAIR = 2 * 10**9, 10**9


def shifted(array, by):
    length = lax.axis_size("blk")
    return lax.ppermute(array, "blk", [(i, (i + by) % length) for i in range(length)])


def normal(raw):
    xf = raw.astype(F32)
    inv = lax.rsqrt(jnp.sum(xf * xf, axis=-1, keepdims=True) + 1e-06)
    return xf * inv, inv


def products(a, b):
    return lax.dot_general(a, b, (((1,), (1,)), ((), ())), preferred_element_type=F32)


def sigmoid(x):
    return 1.0 / (1.0 + jnp.exp(-x))


def fold(v):
    r = jnp.sum(v.reshape(v.shape[0] // 8, 8, v.shape[1]), axis=0)
    return sum(r[:, i : i + 128] for i in range(0, v.shape[1], 128))


def cost(flops):
    return pl.CostEstimate(flops=flops, bytes_accessed=8 << 20, transcendentals=1 << 17)


def add_terms(sums_ref, u, dl, scaled):
    sums_ref[0:8, :] += fold(jnp.maximum(u, 0.0) + jnp.log1p(jnp.exp(-jnp.abs(u))))
    sums_ref[8:16, :] += fold(dl * scaled)
    sums_ref[16:24, :] += fold(dl)


def off_diagonal(own, other, temp, bias, sums_ref=None):
    scaled = temp * products(own, other)
    logit = scaled + bias
    dl = sigmoid(logit)
    if sums_ref is not None:
        add_terms(sums_ref, logit, dl, scaled)
    return (temp * dl).astype(BF16)


def own_kernel(temp_ref, bias_ref, img_ref, txt_ref, img_n_ref, txt_n_ref, gimg_ref, gtxt_ref, sums_ref):
    temp, bias = jnp.exp(temp_ref[...]), bias_ref[...]
    img_n_ref[...] = normal(img_ref[...])[0].astype(BF16)
    txt_n_ref[...] = normal(txt_ref[...])[0].astype(BF16)
    scaled = temp * products(img_n_ref[...], txt_n_ref[...])
    logit = scaled + bias
    rows = lax.broadcasted_iota(jnp.int32, logit.shape, 0)
    cols = lax.broadcasted_iota(jnp.int32, logit.shape, 1)
    diagonal = rows == cols
    u = jnp.where(diagonal, -logit, logit)
    s = sigmoid(u)
    dl = jnp.where(diagonal, -s, s)
    sums_ref[...] = jnp.zeros_like(sums_ref)
    add_terms(sums_ref, u, dl, scaled)
    g = (temp * dl).astype(BF16)
    gimg_ref[...] = jnp.dot(g, txt_n_ref[...], preferred_element_type=F32)
    gtxt_ref[...] = lax.dot_general(
        g, img_n_ref[...], (((0,), (0,)), ((), ())), preferred_element_type=F32
    )


def own_tile(temp, bias, image, text):
    block = image.shape
    return pl.pallas_call(
        own_kernel,
        out_shape=(
            jax.ShapeDtypeStruct(block, BF16),
            jax.ShapeDtypeStruct(block, BF16),
            jax.ShapeDtypeStruct(block, F32),
            jax.ShapeDtypeStruct(block, F32),
            jax.ShapeDtypeStruct((24, 128), F32),
        ),
        compiler_params=pltpu.CompilerParams(vmem_limit_bytes=24 << 20),
        name="own_tile",
    )(temp, bias, image, text)


def pair_kernel(with_older, counted, keep, *refs):
    refs = list(refs)
    temp_ref, bias_ref, img_n_ref, txt_n_ref, t_ref, i_ref, gimg_in, gtxt_in = refs[:8]
    del refs[:8]
    temp, bias = jnp.exp(temp_ref[...]), bias_ref[...]
    older = None
    sums_in = None
    if with_older:
        older = refs.pop(0)
    if counted:
        sums_in = refs.pop(0)
    gimg_ref, gtxt_ref = refs[:2]
    del refs[:2]
    sums_ref = None
    if counted:
        sums_ref = refs.pop(0)
        sums_ref[...] = sums_in[...]
    t_n = normal(t_ref[...])[0].astype(BF16)
    i_n = normal(i_ref[...])[0].astype(BF16)
    if keep:
        refs.pop(0)[...] = i_n
    g = off_diagonal(img_n_ref[...], t_n, temp, bias, sums_ref)
    gimg_ref[...] = gimg_in[...] + jnp.dot(g, t_n, preferred_element_type=F32)
    g = off_diagonal(txt_n_ref[...], i_n, temp, bias)
    gtxt_ref[...] = gtxt_in[...] + jnp.dot(g, i_n, preferred_element_type=F32)
    if older is not None:
        off_diagonal(older[...], t_n, temp, bias, sums_ref)


def pair(temp, bias, own, t, i, acc, sums=None, older=None, keep=False):
    block = t.shape
    args = [temp, bias, *own, t, i, *acc]
    outs = [jax.ShapeDtypeStruct(block, F32)] * 2
    aliases = {6: 0, 7: 1}
    if older is not None:
        args.append(older)
    if sums is not None:
        aliases[len(args)] = len(outs)
        args.append(sums)
        outs.append(jax.ShapeDtypeStruct((24, 128), F32))
    if keep:
        outs.append(jax.ShapeDtypeStruct(block, BF16))
    return pl.pallas_call(
        functools.partial(pair_kernel, older is not None, sums is not None, keep),
        out_shape=tuple(outs),
        input_output_aliases=aliases,
        compiler_params=pltpu.CompilerParams(vmem_limit_bytes=24 << 20),
        cost_estimate=cost(COST_PAIR),
        name="pair",
    )(*args)


def count_kernel(temp_ref, bias_ref, i_ref, t_ref, sums_in, sums_ref):
    temp, bias = jnp.exp(temp_ref[...]), bias_ref[...]
    sums_ref[...] = sums_in[...]
    i_n = normal(i_ref[...])[0].astype(BF16)
    t_n = normal(t_ref[...])[0].astype(BF16)
    off_diagonal(i_n, t_n, temp, bias, sums_ref)


def count(temp, bias, i, t, sums):
    return pl.pallas_call(
        count_kernel,
        out_shape=jax.ShapeDtypeStruct((24, 128), F32),
        input_output_aliases={4: 0},
        compiler_params=pltpu.CompilerParams(vmem_limit_bytes=24 << 20),
        name="count",
    )(temp, bias, i, t, sums)


def last_kernel(temp_ref, bias_ref, img_n_ref, txt_n_ref, t_ref, i_ref, gimg_in, gtxt_in, img_ref, txt_ref, gimg_ref, gtxt_ref):
    temp, bias = jnp.exp(temp_ref[...]), bias_ref[...]
    for own_n, arrived, acc, own, out in (
        (img_n_ref, t_ref, gimg_in, img_ref, gimg_ref),
        (txt_n_ref, i_ref, gtxt_in, txt_ref, gtxt_ref),
    ):
        o_n = normal(arrived[...])[0].astype(BF16)
        g = off_diagonal(own_n[...], o_n, temp, bias)
        grad = acc[...] + jnp.dot(g, o_n, preferred_element_type=F32)
        unit, inv = normal(own[...])
        out[...] = inv * (grad - unit * jnp.sum(unit * grad, axis=-1, keepdims=True))


def last(temp, bias, own, t, i, acc, image, text):
    block = t.shape
    return pl.pallas_call(
        last_kernel,
        out_shape=(jax.ShapeDtypeStruct(block, F32),) * 2,
        compiler_params=pltpu.CompilerParams(vmem_limit_bytes=24 << 20),
        cost_estimate=cost(COST_LAST),
        name="last",
    )(temp, bias, *own, t, i, *acc, image, text)


def spread_kernel(parts_ref, out_ref):
    out_ref[...] = jnp.broadcast_to(jnp.sum(parts_ref[...], axis=0)[None], out_ref.shape)


def spread(parts, copies):
    return pl.pallas_call(
        spread_kernel,
        out_shape=jax.ShapeDtypeStruct((copies,) + parts.shape[1:], F32),
        compiler_params=pltpu.CompilerParams(vmem_limit_bytes=8 << 20),
        name="spread",
    )(parts)


def finish_kernel(pair_count, parts_ref, *out_refs):
    total = jnp.sum(parts_ref[...], axis=0)
    for k, out_ref in enumerate(out_refs):
        out_ref[...] = jnp.sum(total[8 * k : 8 * k + 8], keepdims=True) / pair_count


def finish(parts, pair_count):
    totals = pl.pallas_call(
        functools.partial(finish_kernel, pair_count),
        out_shape=(jax.ShapeDtypeStruct((1, 1), F32),) * 3,
        compiler_params=pltpu.CompilerParams(vmem_limit_bytes=8 << 20),
        name="finish",
    )(parts)
    return tuple(total.reshape(1) for total in totals)


def to_all(parts, axis):
    return lax.all_to_all(parts, axis, 0, 0)


def body(image, text, log_temp, bias):
    temp, shift = log_temp.reshape(1, 1), bias.reshape(1, 1)
    pair_count = image.shape[0] * lax.axis_size("blk") * lax.axis_size("dp")
    after = lax.optimization_barrier
    t, i = {0: text}, {0: image}
    t[1], i[-1] = shifted(text, 1), shifted(image, -1)
    i[1], t[-1] = shifted(image, 1), shifted(text, -1)
    img_n, txt_n, *acc, sums = own_tile(temp, shift, image, text)
    t[1], i[-1], img_n, txt_n = after((t[1], i[-1], img_n, txt_n))
    own = (img_n, txt_n)
    t[2], i[-2] = shifted(t[1], 1), shifted(i[-1], -1)
    *acc, sums, i_m1 = pair(temp, shift, own, t[1], i[-1], acc, sums, keep=True)
    i[1], t[-1], sums = after((i[1], t[-1], sums))
    i[2], t[-2] = shifted(i[1], 1), shifted(t[-1], -1)
    *acc, sums, i_1 = pair(temp, shift, own, t[-1], i[1], acc, sums, keep=True)
    t[2], i[-2], sums = after((t[2], i[-2], sums))
    t[3], i[-3] = shifted(t[2], 1), shifted(i[-2], -1)
    *acc, sums = pair(temp, shift, own, t[2], i[-2], acc, sums, older=i_m1)
    sums = count(temp, shift, i[-2], t[2], sums)
    i[2], t[-2], sums = after((i[2], t[-2], sums))
    i[3], t[-3] = shifted(i[2], 1), shifted(t[-2], -1)
    *acc, sums = pair(temp, shift, own, t[-2], i[2], acc, sums, older=i_1)
    parts = to_all(spread(sums[None], lax.axis_size("dp")), "dp")
    t[4], i[-4] = shifted(t[3], 1), shifted(i[-3], -1)
    i[3], t[-3], parts = after((i[3], t[-3], parts))
    parts = to_all(spread(parts, lax.axis_size("blk")), "blk")
    acc = pair(temp, shift, own, t[3], i[-3], acc)
    acc = pair(temp, shift, own, t[-3], i[3], acc)
    grad_image, grad_text = last(temp, shift, own, t[4], i[-4], acc, image, text)
    return (*finish(parts, pair_count), grad_image, grad_text)


def solution(mesh):
    placed = (P(("blk", "dp"), None), P(("blk", "dp"), None), P(), P())
    return jax.shard_map(
        body,
        mesh=mesh,
        in_specs=placed,
        out_specs=(P(), P(), P(), P(("blk", "dp"), None), P(("blk", "dp"), None)),
        check_vma=False,
    )
```

```python
import functools

import jax
import jax.numpy as jnp
from jax import lax
from jax.experimental import pallas as pl
from jax.experimental.pallas import tpu as pltpu
from jax.sharding import PartitionSpec as P

F32, BF16 = jnp.float32, jnp.bfloat16
COST_LAST, COST_PAIR, COST_FINISH = 2 * 10**9, 10**9, 115 * 10**9


def shifted(array, by):
    length = lax.axis_size("blk")
    return lax.ppermute(array, "blk", [(i, (i + by) % length) for i in range(length)])


def normal(raw):
    xf = raw.astype(F32)
    inv = lax.rsqrt(jnp.sum(xf * xf, axis=-1, keepdims=True) + 1e-06)
    return xf * inv, inv


def products(a, b):
    return lax.dot_general(a, b, (((1,), (1,)), ((), ())), preferred_element_type=F32)


def sigmoid(x):
    return 1.0 / (1.0 + jnp.exp(-x))


def fold(v):
    r = jnp.sum(v.reshape(v.shape[0] // 8, 8, v.shape[1]), axis=0)
    return sum(r[:, i : i + 128] for i in range(0, v.shape[1], 128))


def cost(flops):
    return pl.CostEstimate(flops=flops, bytes_accessed=8 << 20, transcendentals=1 << 17)


def add_terms(sums_ref, u, dl, scaled):
    sums_ref[0:8, :] += fold(jnp.maximum(u, 0.0) + jnp.log1p(jnp.exp(-jnp.abs(u))))
    sums_ref[8:16, :] += fold(dl * scaled)
    sums_ref[16:24, :] += fold(dl)


def off_diagonal(own, other, temp, bias, sums_ref=None):
    scaled = temp * products(own, other)
    logit = scaled + bias
    dl = sigmoid(logit)
    if sums_ref is not None:
        add_terms(sums_ref, logit, dl, scaled)
    return (temp * dl).astype(BF16)


def own_kernel(temp_ref, bias_ref, img_ref, txt_ref, img_n_ref, txt_n_ref, gimg_ref, gtxt_ref, sums_ref):
    temp, bias = jnp.exp(temp_ref[...]), bias_ref[...]
    img_n_ref[...] = normal(img_ref[...])[0].astype(BF16)
    txt_n_ref[...] = normal(txt_ref[...])[0].astype(BF16)
    scaled = temp * products(img_n_ref[...], txt_n_ref[...])
    logit = scaled + bias
    rows = lax.broadcasted_iota(jnp.int32, logit.shape, 0)
    cols = lax.broadcasted_iota(jnp.int32, logit.shape, 1)
    diagonal = rows == cols
    u = jnp.where(diagonal, -logit, logit)
    s = sigmoid(u)
    dl = jnp.where(diagonal, -s, s)
    sums_ref[...] = jnp.zeros_like(sums_ref)
    add_terms(sums_ref, u, dl, scaled)
    g = (temp * dl).astype(BF16)
    gimg_ref[...] = jnp.dot(g, txt_n_ref[...], preferred_element_type=F32)
    gtxt_ref[...] = lax.dot_general(
        g, img_n_ref[...], (((0,), (0,)), ((), ())), preferred_element_type=F32
    )


def own_tile(temp, bias, image, text):
    block = image.shape
    return pl.pallas_call(
        own_kernel,
        out_shape=(
            jax.ShapeDtypeStruct(block, BF16),
            jax.ShapeDtypeStruct(block, BF16),
            jax.ShapeDtypeStruct(block, F32),
            jax.ShapeDtypeStruct(block, F32),
            jax.ShapeDtypeStruct((24, 128), F32),
        ),
        compiler_params=pltpu.CompilerParams(vmem_limit_bytes=24 << 20),
        name="own_tile",
    )(temp, bias, image, text)


def pair_kernel(with_older, crossed, counted, keep, *refs):
    refs = list(refs)
    temp_ref, bias_ref, img_n_ref, txt_n_ref, t_ref, i_ref, gimg_in, gtxt_in = refs[:8]
    del refs[:8]
    temp, bias = jnp.exp(temp_ref[...]), bias_ref[...]
    older = None
    sums_in = None
    if with_older:
        older = refs.pop(0)
    if counted:
        sums_in = refs.pop(0)
    gimg_ref, gtxt_ref = refs[:2]
    del refs[:2]
    sums_ref = None
    if counted:
        sums_ref = refs.pop(0)
        sums_ref[...] = sums_in[...]
    t_n = normal(t_ref[...])[0].astype(BF16)
    i_n = normal(i_ref[...])[0].astype(BF16)
    if keep:
        refs.pop(0)[...] = i_n
    g = off_diagonal(img_n_ref[...], t_n, temp, bias, sums_ref)
    gimg_ref[...] = gimg_in[...] + jnp.dot(g, t_n, preferred_element_type=F32)
    g = off_diagonal(txt_n_ref[...], i_n, temp, bias)
    gtxt_ref[...] = gtxt_in[...] + jnp.dot(g, i_n, preferred_element_type=F32)
    if older is not None:
        off_diagonal(older[...], t_n, temp, bias, sums_ref)
    if crossed:
        off_diagonal(i_n, t_n, temp, bias, sums_ref)


def pair(temp, bias, own, t, i, acc, sums=None, older=None, crossed=False, keep=False):
    block = t.shape
    args = [temp, bias, *own, t, i, *acc]
    outs = [jax.ShapeDtypeStruct(block, F32)] * 2
    aliases = {6: 0, 7: 1}
    if older is not None:
        args.append(older)
    if sums is not None:
        aliases[len(args)] = len(outs)
        args.append(sums)
        outs.append(jax.ShapeDtypeStruct((24, 128), F32))
    if keep:
        outs.append(jax.ShapeDtypeStruct(block, BF16))
    return pl.pallas_call(
        functools.partial(pair_kernel, older is not None, crossed, sums is not None, keep),
        out_shape=tuple(outs),
        input_output_aliases=aliases,
        compiler_params=pltpu.CompilerParams(vmem_limit_bytes=24 << 20),
        cost_estimate=cost(COST_PAIR),
        name="pair",
    )(*args)


def last_kernel(temp_ref, bias_ref, img_n_ref, txt_n_ref, t_ref, i_ref, gimg_in, gtxt_in, img_ref, txt_ref, gimg_ref, gtxt_ref):
    temp, bias = jnp.exp(temp_ref[...]), bias_ref[...]
    for own_n, arrived, acc, own, out in (
        (img_n_ref, t_ref, gimg_in, img_ref, gimg_ref),
        (txt_n_ref, i_ref, gtxt_in, txt_ref, gtxt_ref),
    ):
        o_n = normal(arrived[...])[0].astype(BF16)
        g = off_diagonal(own_n[...], o_n, temp, bias)
        grad = acc[...] + jnp.dot(g, o_n, preferred_element_type=F32)
        unit, inv = normal(own[...])
        out[...] = inv * (grad - unit * jnp.sum(unit * grad, axis=-1, keepdims=True))


def last(temp, bias, own, t, i, acc, image, text):
    block = t.shape
    return pl.pallas_call(
        last_kernel,
        out_shape=(jax.ShapeDtypeStruct(block, F32),) * 2,
        compiler_params=pltpu.CompilerParams(vmem_limit_bytes=24 << 20),
        cost_estimate=cost(COST_LAST),
        name="last",
    )(temp, bias, *own, t, i, *acc, image, text)


def spread_kernel(parts_ref, out_ref):
    out_ref[...] = jnp.broadcast_to(jnp.sum(parts_ref[...], axis=0)[None], out_ref.shape)


def spread(parts, copies):
    return pl.pallas_call(
        spread_kernel,
        out_shape=jax.ShapeDtypeStruct((copies,) + parts.shape[1:], F32),
        compiler_params=pltpu.CompilerParams(vmem_limit_bytes=8 << 20),
        name="spread",
    )(parts)


def finish_kernel(pair_count, parts_ref, *out_refs):
    total = jnp.sum(parts_ref[...], axis=0)
    for k, out_ref in enumerate(out_refs):
        out_ref[...] = jnp.sum(total[8 * k : 8 * k + 8], keepdims=True) / pair_count


def finish(parts, pair_count):
    totals = pl.pallas_call(
        functools.partial(finish_kernel, pair_count),
        out_shape=(jax.ShapeDtypeStruct((1, 1), F32),) * 3,
        compiler_params=pltpu.CompilerParams(vmem_limit_bytes=8 << 20),
        cost_estimate=cost(COST_FINISH),
        name="finish",
    )(parts)
    return tuple(total.reshape(1) for total in totals)


def to_all(parts, axis):
    return lax.all_to_all(parts, axis, 0, 0)


def body(image, text, log_temp, bias):
    temp, shift = log_temp.reshape(1, 1), bias.reshape(1, 1)
    pair_count = image.shape[0] * lax.axis_size("blk") * lax.axis_size("dp")
    after = lax.optimization_barrier
    t, i = {0: text}, {0: image}
    t[1], i[-1] = shifted(text, 1), shifted(image, -1)
    t[-1], i[1] = shifted(text, -1), shifted(image, 1)
    img_n, txt_n, *acc, sums = own_tile(temp, shift, image, text)
    t[1], img_n, txt_n = after((t[1], img_n, txt_n))
    own = (img_n, txt_n)
    t[2] = shifted(t[1], 1)
    *acc, sums, i_m1 = pair(temp, shift, own, t[1], i[-1], acc, sums, keep=True)
    i[-1], sums = after((i[-1], sums))
    i[-2] = shifted(i[-1], -1)
    t[-2] = shifted(t[-1], -1)
    *acc, sums, i_1 = pair(temp, shift, own, t[-1], i[1], acc, sums, keep=True)
    i[1], sums = after((i[1], sums))
    i[2] = shifted(i[1], 1)
    t[3] = shifted(t[2], 1)
    *acc, sums = pair(temp, shift, own, t[2], i[-2], acc, sums, older=i_m1, crossed=True)
    i[-2], sums = after((i[-2], sums))
    i[-3] = shifted(i[-2], -1)
    t[-3] = shifted(t[-2], -1)
    *acc, sums = pair(temp, shift, own, t[-2], i[2], acc, sums, older=i_1)
    i[2], sums = after((i[2], sums))
    i[3] = shifted(i[2], 1)
    parts = to_all(spread(sums[None], lax.axis_size("dp")), "dp")
    t[4], i[-4] = shifted(t[3], 1), shifted(i[-3], -1)
    i[3], t[-3], parts = after((i[3], t[-3], parts))
    parts = to_all(spread(parts, lax.axis_size("blk")), "blk")
    acc = pair(temp, shift, own, t[3], i[-3], acc)
    acc = pair(temp, shift, own, t[-3], i[3], acc)
    grad_image, grad_text = last(temp, shift, own, t[4], i[-4], acc, image, text)
    return (*finish(parts, pair_count), grad_image, grad_text)


def solution(mesh):
    placed = (P(("blk", "dp"), None), P(("blk", "dp"), None), P(), P())
    return jax.shard_map(
        body,
        mesh=mesh,
        in_specs=placed,
        out_specs=(P(), P(), P(), P(("blk", "dp"), None), P(("blk", "dp"), None)),
        check_vma=False,
    )
```

```python
import functools

import jax
import jax.numpy as jnp
from jax import lax
from jax.experimental import pallas as pl
from jax.experimental.pallas import tpu as pltpu
from jax.sharding import PartitionSpec as P

F32, BF16 = jnp.float32, jnp.bfloat16
COST_LAST, COST_PAIR, COST_FINISH = 2 * 10**9, 10**9, 115 * 10**9


def shifted(array, by):
    length = lax.axis_size("blk")
    return lax.ppermute(array, "blk", [(i, (i + by) % length) for i in range(length)])


def normal(raw):
    xf = raw.astype(F32)
    inv = lax.rsqrt(jnp.sum(xf * xf, axis=-1, keepdims=True) + 1e-06)
    return xf * inv, inv


def products(a, b):
    return lax.dot_general(a, b, (((1,), (1,)), ((), ())), preferred_element_type=F32)


def sigmoid(x):
    return 1.0 / (1.0 + jnp.exp(-x))


def fold(v):
    r = jnp.sum(v.reshape(v.shape[0] // 8, 8, v.shape[1]), axis=0)
    return sum(r[:, i : i + 128] for i in range(0, v.shape[1], 128))


def cost(flops):
    return pl.CostEstimate(flops=flops, bytes_accessed=8 << 20, transcendentals=1 << 17)


def add_terms(sums_ref, u, dl, scaled):
    sums_ref[0:8, :] += fold(jnp.maximum(u, 0.0) + jnp.log1p(jnp.exp(-jnp.abs(u))))
    sums_ref[8:16, :] += fold(dl * scaled)
    sums_ref[16:24, :] += fold(dl)


def off_diagonal(own, other, temp, bias, sums_ref=None):
    scaled = temp * products(own, other)
    logit = scaled + bias
    dl = sigmoid(logit)
    if sums_ref is not None:
        add_terms(sums_ref, logit, dl, scaled)
    return (temp * dl).astype(BF16)


def own_kernel(temp_ref, bias_ref, img_ref, txt_ref, img_n_ref, txt_n_ref, gimg_ref, gtxt_ref, sums_ref):
    temp, bias = jnp.exp(temp_ref[...]), bias_ref[...]
    img_n_ref[...] = normal(img_ref[...])[0].astype(BF16)
    txt_n_ref[...] = normal(txt_ref[...])[0].astype(BF16)
    scaled = temp * products(img_n_ref[...], txt_n_ref[...])
    logit = scaled + bias
    rows = lax.broadcasted_iota(jnp.int32, logit.shape, 0)
    cols = lax.broadcasted_iota(jnp.int32, logit.shape, 1)
    diagonal = rows == cols
    u = jnp.where(diagonal, -logit, logit)
    s = sigmoid(u)
    dl = jnp.where(diagonal, -s, s)
    sums_ref[...] = jnp.zeros_like(sums_ref)
    add_terms(sums_ref, u, dl, scaled)
    g = (temp * dl).astype(BF16)
    gimg_ref[...] = jnp.dot(g, txt_n_ref[...], preferred_element_type=F32)
    gtxt_ref[...] = lax.dot_general(
        g, img_n_ref[...], (((0,), (0,)), ((), ())), preferred_element_type=F32
    )


def own_tile(temp, bias, image, text):
    block = image.shape
    return pl.pallas_call(
        own_kernel,
        out_shape=(
            jax.ShapeDtypeStruct(block, BF16),
            jax.ShapeDtypeStruct(block, BF16),
            jax.ShapeDtypeStruct(block, F32),
            jax.ShapeDtypeStruct(block, F32),
            jax.ShapeDtypeStruct((24, 128), F32),
        ),
        compiler_params=pltpu.CompilerParams(vmem_limit_bytes=24 << 20),
        name="own_tile",
    )(temp, bias, image, text)


def pair_kernel(with_older, crossed, counted, keep, *refs):
    refs = list(refs)
    temp_ref, bias_ref, img_n_ref, txt_n_ref, t_ref, i_ref, gimg_in, gtxt_in = refs[:8]
    del refs[:8]
    temp, bias = jnp.exp(temp_ref[...]), bias_ref[...]
    older = None
    sums_in = None
    if with_older:
        older = refs.pop(0)
    if counted:
        sums_in = refs.pop(0)
    gimg_ref, gtxt_ref = refs[:2]
    del refs[:2]
    sums_ref = None
    if counted:
        sums_ref = refs.pop(0)
        sums_ref[...] = sums_in[...]
    t_n = normal(t_ref[...])[0].astype(BF16)
    i_n = normal(i_ref[...])[0].astype(BF16)
    if keep:
        refs.pop(0)[...] = i_n
    g = off_diagonal(img_n_ref[...], t_n, temp, bias, sums_ref)
    gimg_ref[...] = gimg_in[...] + jnp.dot(g, t_n, preferred_element_type=F32)
    g = off_diagonal(txt_n_ref[...], i_n, temp, bias)
    gtxt_ref[...] = gtxt_in[...] + jnp.dot(g, i_n, preferred_element_type=F32)
    if older is not None:
        off_diagonal(older[...], t_n, temp, bias, sums_ref)
    if crossed:
        off_diagonal(i_n, t_n, temp, bias, sums_ref)


def pair(temp, bias, own, t, i, acc, sums=None, older=None, crossed=False, keep=False):
    block = t.shape
    args = [temp, bias, *own, t, i, *acc]
    outs = [jax.ShapeDtypeStruct(block, F32)] * 2
    aliases = {6: 0, 7: 1}
    if older is not None:
        args.append(older)
    if sums is not None:
        aliases[len(args)] = len(outs)
        args.append(sums)
        outs.append(jax.ShapeDtypeStruct((24, 128), F32))
    if keep:
        outs.append(jax.ShapeDtypeStruct(block, BF16))
    return pl.pallas_call(
        functools.partial(pair_kernel, older is not None, crossed, sums is not None, keep),
        out_shape=tuple(outs),
        input_output_aliases=aliases,
        compiler_params=pltpu.CompilerParams(vmem_limit_bytes=24 << 20),
        cost_estimate=cost(COST_PAIR),
        name="pair",
    )(*args)


def last_kernel(temp_ref, bias_ref, img_n_ref, txt_n_ref, t_ref, i_ref, gimg_in, gtxt_in, img_ref, txt_ref, gimg_ref, gtxt_ref):
    temp, bias = jnp.exp(temp_ref[...]), bias_ref[...]
    for own_n, arrived, acc, own, out in (
        (img_n_ref, t_ref, gimg_in, img_ref, gimg_ref),
        (txt_n_ref, i_ref, gtxt_in, txt_ref, gtxt_ref),
    ):
        o_n = normal(arrived[...])[0].astype(BF16)
        g = off_diagonal(own_n[...], o_n, temp, bias)
        grad = acc[...] + jnp.dot(g, o_n, preferred_element_type=F32)
        unit, inv = normal(own[...])
        out[...] = inv * (grad - unit * jnp.sum(unit * grad, axis=-1, keepdims=True))


def last(temp, bias, own, t, i, acc, image, text):
    block = t.shape
    return pl.pallas_call(
        last_kernel,
        out_shape=(jax.ShapeDtypeStruct(block, F32),) * 2,
        compiler_params=pltpu.CompilerParams(vmem_limit_bytes=24 << 20),
        cost_estimate=cost(COST_LAST),
        name="last",
    )(temp, bias, *own, t, i, *acc, image, text)


def spread_kernel(parts_ref, out_ref):
    out_ref[...] = jnp.broadcast_to(jnp.sum(parts_ref[...], axis=0)[None], out_ref.shape)


def spread(parts, copies):
    return pl.pallas_call(
        spread_kernel,
        out_shape=jax.ShapeDtypeStruct((copies,) + parts.shape[1:], F32),
        compiler_params=pltpu.CompilerParams(vmem_limit_bytes=8 << 20),
        name="spread",
    )(parts)


def finish_kernel(pair_count, parts_ref, *out_refs):
    total = jnp.sum(parts_ref[...], axis=0)
    for k, out_ref in enumerate(out_refs):
        out_ref[...] = jnp.sum(total[8 * k : 8 * k + 8], keepdims=True) / pair_count


def finish(parts, pair_count):
    totals = pl.pallas_call(
        functools.partial(finish_kernel, pair_count),
        out_shape=(jax.ShapeDtypeStruct((1, 1), F32),) * 3,
        compiler_params=pltpu.CompilerParams(vmem_limit_bytes=8 << 20),
        cost_estimate=cost(COST_FINISH),
        name="finish",
    )(parts)
    return tuple(total.reshape(1) for total in totals)


def to_all(parts, axis):
    return lax.all_to_all(parts, axis, 0, 0)


def body(image, text, log_temp, bias):
    temp, shift = log_temp.reshape(1, 1), bias.reshape(1, 1)
    pair_count = image.shape[0] * lax.axis_size("blk") * lax.axis_size("dp")
    after = lax.optimization_barrier
    t, i = {0: text}, {0: image}
    t[1], i[-1] = shifted(text, 1), shifted(image, -1)
    t[-1], i[1] = shifted(text, -1), shifted(image, 1)
    img_n, txt_n, *acc, sums = own_tile(temp, shift, image, text)
    t[1], img_n, txt_n = after((t[1], img_n, txt_n))
    own = (img_n, txt_n)
    t[2] = shifted(t[1], 1)
    *acc, sums, i_m1 = pair(temp, shift, own, t[1], i[-1], acc, sums, keep=True)
    i[-1], sums = after((i[-1], sums))
    i[-2] = shifted(i[-1], -1)
    t[-2] = shifted(t[-1], -1)
    *acc, sums, i_1 = pair(temp, shift, own, t[-1], i[1], acc, sums, keep=True)
    i[1], sums = after((i[1], sums))
    i[2] = shifted(i[1], 1)
    t[3] = shifted(t[2], 1)
    *acc, sums = pair(temp, shift, own, t[2], i[-2], acc, sums, older=i_m1, crossed=True)
    i[-2], sums = after((i[-2], sums))
    i[-3] = shifted(i[-2], -1)
    t[-3] = shifted(t[-2], -1)
    *acc, sums = pair(temp, shift, own, t[-2], i[2], acc, sums, older=i_1)
    i[2], sums = after((i[2], sums))
    i[3] = shifted(i[2], 1)
    parts = to_all(spread(sums[None], lax.axis_size("dp")), "dp")
    t[4], i[-4] = shifted(t[3], 1), shifted(i[-3], -1)
    acc = pair(temp, shift, own, t[3], i[-3], acc)
    acc, i[3], t[-3], parts = after((acc, i[3], t[-3], parts))
    parts = to_all(spread(parts, lax.axis_size("blk")), "blk")
    acc = pair(temp, shift, own, t[-3], i[3], acc)
    grad_image, grad_text = last(temp, shift, own, t[4], i[-4], acc, image, text)
    return (*finish(parts, pair_count), grad_image, grad_text)


def solution(mesh):
    placed = (P(("blk", "dp"), None), P(("blk", "dp"), None), P(), P())
    return jax.shard_map(
        body,
        mesh=mesh,
        in_specs=placed,
        out_specs=(P(), P(), P(), P(("blk", "dp"), None), P(("blk", "dp"), None)),
        check_vma=False,
    )
```
